256 devices in a mesh: dp: 128 (over x, z, y), hid: 2 (over core).
Axes of the slice: x: 4, y: 4, z: 8, core: 2. Of those that a mesh axis runs over, the one named last changes fastest.
Arguments:
- tokens: bfloat16 [16384, 3584], P('dp', 'hid'), may hold values from -6 to 6
- routes: int32 [16384, 8], P('dp'), may hold values from 0 to 127, all different within a row; in each aligned block of 128 rows (0 to 127, 128 to 255, ...) at most 9 rows name the same one
- gates: float32 [16384, 8], P('dp'), may hold values from 0.05 to 1
- capacity: int32 [128], replicated, may hold values from 288 to 1152, as said below
- w_gate: bfloat16 [128, 3584, 1024], P('dp', None, 'hid'), may hold values from -0.09375 to 0.09375
- w_up: bfloat16 [128, 3584, 1024], P('dp', None, 'hid'), may hold values from -0.09375 to 0.09375
- w_down: bfloat16 [128, 1024, 3584], P('dp', 'hid'), may hold values from -0.1875 to 0.1875
Outputs:
- mixed_out: bfloat16 [16384, 3584], P('dp', 'hid')
The draws below stay inside these ranges and needn't reach their ends.
Inputs may be any that keep to these rules, and one draw needn't show every extreme that they name: `routes`: each row names 8 different experts; no expert is named by more than 9 rows of one index of dp's 128 rows. Some expert has capacity exactly 1152.
All inputs are finite; a program needn't handle non-finite values.
Results may differ from the reference program's by a relative error of at most 0.0063.
Values may be sent and summed in bfloat16 or wider, within the bound.
No kernel may reach another device: no remote copies, remote signals or barrier semaphores. Data moves between devices by JAX's collectives and lax.ppermute only.
A program may use at most 192 MiB of HBM per device.

```python
import math
import jax
import jax.numpy as jnp
import numpy as np
from jax import lax

D = 3584
FF = 1024
TOP = 8
TOK_DEV = 128
EXPERTS = 128
TOKENS = 16384
S = 9
N_DP = 128


def draw_capacity(key, part):
    key = jax.random.fold_in(key, 7)
    first_key, second_key = jax.random.split(key)
    highest = EXPERTS * S
    lowest = highest // 4
    upper = highest * 3 // 4
    values = jax.random.randint(first_key, (EXPERTS,), lowest, upper + 1)
    chosen = jax.random.randint(second_key, (), 0, EXPERTS)
    return jnp.where(jnp.arange(EXPERTS) == chosen, highest, values).astype(jnp.int32)


def steps_of(rng, dims, cuts, least, top_value):
    gain, own = 1.0, jax.random.fold_in(rng, 6)
    for position, blocks in cuts:
        draws = jnp.exp(jax.random.uniform(jax.random.fold_in(own, position), (blocks,), jnp.float32, least / len(cuts), top_value / len(cuts)))
        gain = gain * jnp.repeat(draws, dims[position] // blocks).reshape([-1 if axis == position else 1 for axis in range(len(dims))])
    return gain


def routed_block(key, own, number, rows, number_of, top, limit, slope):
    order = jax.random.permutation(key, number_of)
    packed, common = shares(number_of, rows * top, limit, slope, True), shares(number_of, rows * top, limit, slope, False)
    places = jnp.arange(number_of)

    def named(tallies, turn):
        used = int((tallies > 0).sum())
        fixed = max(1, used // 4)
        moved = fixed + (places - fixed + turn * (used - fixed)) % max(1, number_of - fixed)
        return jnp.zeros((number_of,), jnp.int32).at[order[jnp.where(places < fixed, places, moved)]].set(jnp.asarray(tallies, jnp.int32))

    tallies = jnp.where(number % 4 == 0, named(packed, number // 4), named(common, number - number // 4 - 1))
    mixed = jax.random.permutation(jax.random.fold_in(own, 3), number_of)
    donor, taker = mixed[0:number_of // 2 * 2:2], mixed[1:number_of // 2 * 2:2]
    margin = jnp.minimum(tallies[donor] - 1, limit - tallies[taker]) // 2
    margin = jnp.where((donor == order[0]) | (taker == order[0]) | (tallies[taker] == 0), 0, jnp.maximum(margin, 0))
    moved = jax.random.randint(jax.random.fold_in(own, 4), (number_of // 2,), 0, 1 << 20) % (margin + 1)
    tallies = tallies.at[donor].add(-moved).at[taker].add(moved)
    items = jnp.searchsorted(jnp.cumsum(tallies), jnp.arange(rows * top), side="right").astype(jnp.int32)
    table = items.reshape(top, rows).T
    table = table[jax.random.permutation(jax.random.fold_in(own, 1), rows)]
    turn = jax.random.randint(jax.random.fold_in(own, 2), (rows, 1), 0, top)
    return jnp.take_along_axis(table, (jnp.arange(top)[None, :] + turn) % top, axis=1)


def shares(number_of, total, bound, skew, full):
    loads = [(1 << 20) // math.isqrt(standing ** skew) + 1 for standing in range(1, number_of + 1)]
    largest = bound if full else min(bound, max(-(-total // number_of), total * loads[0] // sum(loads)))
    least = 1 if total - largest >= number_of - 1 else 0
    holding, rest = [largest] + [least] * (number_of - 1), total - largest - least * (number_of - 1)
    while rest > 0:
        free = [i for i in range(1, number_of) if holding[i] < largest] or [i for i in range(1, number_of) if holding[i] < bound]
        pool, budget = sum([loads[i] for i in free]), rest
        for i in free:
            more = min(bound - holding[i], max(1, budget * loads[i] // pool), rest)
            holding[i] = holding[i] + more
            rest = rest - more
    return np.array(holding)


def centred(rng, dims, scale, reach, cuts=(), held_as=jnp.bfloat16):
    array = scale * jax.random.normal(rng, dims, jnp.float32)
    if cuts:
        array = array * steps_of(rng, dims, cuts, -0.22, 0.18)
    return jnp.clip(array, -reach, reach).astype(held_as)


def setup_inputs(seed: int = 0) -> dict:
    seeds = jax.random.split(jax.random.key(seed), 8)
    tokens = centred(seeds[0], (TOKENS, D), 1.0, 6.0, ((0, 128), (1, 2)))
    routes_keys = jax.random.split(jax.random.fold_in(seeds[1], 1), TOKENS // TOK_DEV)
    routes_turns = jax.random.permutation(jax.random.fold_in(seeds[1], 3), TOKENS // TOK_DEV)
    routes = jax.vmap(lambda own, number: routed_block(jax.random.fold_in(seeds[1], 2), own, number, TOK_DEV, EXPERTS, TOP, S, 1))(routes_keys, routes_turns).reshape((TOKENS, TOP))
    gates = jnp.clip(0.05 + 0.95 * jax.random.uniform(seeds[2], (TOKENS, TOP), jnp.float32) ** steps_of(seeds[2], (TOKENS, TOP), ((0, 128),), -0.2, 0.2), 0.05, 1.0)
    capacity = draw_capacity(jax.random.fold_in(seeds[7], 71), 0)
    w_gate = centred(seeds[4], (EXPERTS, D, FF), D ** -0.5, 0.09375, ((0, 128), (2, 2)))
    w_up = centred(seeds[5], (EXPERTS, D, FF), D ** -0.5, 0.09375, ((0, 128), (2, 2)))
    w_down = centred(seeds[6], (EXPERTS, FF, D), FF ** -0.5, 0.1875, ((0, 128), (1, 2)))
    return {"tokens": tokens, "routes": routes, "gates": gates, "capacity": capacity, "w_gate": w_gate, "w_up": w_up, "w_down": w_down}


def reference(tokens, routes, gates, capacity, w_gate, w_up, w_down):
    slot_total = EXPERTS * S
    labels = jnp.arange(EXPERTS, dtype=jnp.int32)
    blocks = routes.reshape(N_DP, TOK_DEV * TOP)

    def rank_block(running, block_routes):
        one_hot = (block_routes[:, None] == labels[None, :]).astype(jnp.int32)
        earlier = (jnp.cumsum(one_hot, axis=0, dtype=jnp.int32) - one_hot).astype(jnp.int32)
        route_rank = jnp.sum(one_hot * (earlier + running[None, :]), axis=1, dtype=jnp.int32).astype(jnp.int32)
        updated = (running + jnp.sum(one_hot, axis=0, dtype=jnp.int32)).astype(jnp.int32)
        return updated, route_rank

    _, route_rank = lax.scan(rank_block, jnp.zeros((EXPERTS,), jnp.int32), blocks)
    route_rank = route_rank.reshape(TOKENS * TOP)
    flat_routes = routes.reshape(TOKENS * TOP)
    is_kept = route_rank < capacity[flat_routes]
    rounded = lax.optimization_barrier(gates.astype(jnp.bfloat16)).astype(jnp.float32).reshape(TOKENS * TOP)
    combine = jnp.where(is_kept, rounded, jnp.zeros_like(rounded))
    owners = (jnp.arange(TOKENS * TOP, dtype=jnp.int32) // TOP).astype(jnp.int32)

    def one_expert(running_out, expert_id):
        matched = flat_routes == expert_id
        route_index = jnp.nonzero(matched, size=slot_total, fill_value=0)[0].astype(jnp.int32)
        is_valid = jnp.arange(slot_total, dtype=jnp.int32) < jnp.sum(matched.astype(jnp.int32), dtype=jnp.int32)
        token_index = owners[route_index]
        row_block = tokens[token_index]
        gate_part = jnp.dot(row_block, w_gate[expert_id], preferred_element_type=jnp.float32)
        up_part = jnp.dot(row_block, w_up[expert_id], preferred_element_type=jnp.float32)
        hidden = (jax.nn.silu(gate_part) * up_part).astype(jnp.bfloat16)
        expert_out = jnp.dot(hidden, w_down[expert_id], preferred_element_type=jnp.float32).astype(jnp.bfloat16)
        factor = jnp.where(is_valid, combine[route_index], jnp.zeros((slot_total,), combine.dtype))
        added = (factor[:, None] * expert_out.astype(jnp.float32)).astype(running_out.dtype)
        running_out = running_out.at[token_index].add(added)
        return running_out, None

    mixed_out, _ = lax.scan(one_expert, jnp.zeros((TOKENS, D), jnp.float32), labels)
    return mixed_out.astype(jnp.bfloat16)
```

```python
import jax
import jax.numpy as jnp
from jax import lax
from jax.sharding import Mesh, PartitionSpec as P

NX, NZ, NY = 4, 8, 4
SLOTS = 9
BF = jnp.bfloat16
F32 = jnp.float32
SWAP = ((0, 1), (1, 0))


def shift(size, by):
    return [(i, (i + by) % size) for i in range(size)]


def ring_gather(block):
    up, down = [block], [block]
    for step in range(4):
        up.append(lax.ppermute(up[-1], "z", shift(NZ, 1)))
        if step < 3:
            down.append(lax.ppermute(down[-1], "z", shift(NZ, -1)))
    return up + down[:0:-1]


def ring_scatter(part):
    down, up = part[4], part[5]
    for k in (3, 2, 1):
        down = lax.ppermute(down.astype(BF), "z", shift(NZ, -1)).astype(F32) + part[k]
    for k in (6, 7):
        up = lax.ppermute(up.astype(BF), "z", shift(NZ, 1)).astype(F32) + part[k]
    down = lax.ppermute(down.astype(BF), "z", shift(NZ, -1)).astype(F32)
    up = lax.ppermute(up.astype(BF), "z", shift(NZ, 1)).astype(F32)
    return part[0] + down + up


def direct_gather(block, axis, size):
    return [block] + [lax.ppermute(block, axis, shift(size, k)) for k in range(1, size)]


def on_device(tokens, routes, gates, capacity, w_gate, w_up, w_down):
    tok, width = tokens.shape
    planes = NX * NY
    group = SLOTS * NZ
    rows = planes * group
    half = w_gate.shape[2]
    x, z, y, hid = (lax.axis_index(a) for a in ("x", "z", "y", "hid"))
    plane = x * NY + y

    rounded = gates.astype(BF).astype(F32)
    meta = jnp.concatenate([routes.astype(F32), rounded], axis=1).T
    metas = jnp.stack(direct_gather(meta, "z", NZ), axis=1)
    back = jnp.arange(NZ, dtype=jnp.int32)
    source_of = (z - back) % NZ

    experts = jnp.arange(planes, dtype=jnp.int32)
    expert_of = (experts // NY) * (NZ * NY) + z * NY + experts % NY
    named = metas[None, :8] == expert_of[:, None, None, None].astype(F32)
    mask = jnp.any(named, axis=1)
    factor = jnp.sum(jnp.where(named, metas[None, 8:], 0.0), axis=1)
    before = (jnp.arange(tok)[:, None] < jnp.arange(tok)[None, :]).astype(BF)
    earlier = jnp.dot(mask.astype(BF).reshape(planes * NZ, tok), before, preferred_element_type=F32)
    place = jnp.where(mask, earlier.reshape(planes, NZ, tok).astype(jnp.int32), -1)
    sent = jnp.sum(mask.astype(jnp.int32), axis=2)

    ranks = jnp.arange(SLOTS, dtype=jnp.int32)
    same = back[:, None] == source_of[None, :]
    hit = (place[:, None, None] == ranks[None, :, None, None, None]) & same[None, None, :, :, None]
    pick = hit.astype(BF).reshape(rows, NZ * tok)
    merge = jnp.where(hit, factor[:, None, None], 0.0).astype(BF).reshape(rows, NZ * tok)

    sent = jnp.sum(jnp.where(same[None], sent[:, None, :], 0), axis=2)
    along_x = jnp.stack(direct_gather(sent, "x", NX))
    along_xy = jnp.stack(direct_gather(along_x, "y", NY))
    mine = jnp.sum(jnp.where(experts[None, None, :, None] == plane, along_xy, 0), axis=2)
    src_x = (x - jnp.arange(NX)) % NX
    src_y = (y - jnp.arange(NY)) % NY
    order = (src_x[None, :, None] * NZ + back[None, None, :]) * NY + src_y[:, None, None]
    own_order = ((experts // NY)[:, None] * NZ + back[None, :]) * NY + (experts % NY)[:, None]
    ahead = order.reshape(1, 1, -1) < own_order[:, :, None]
    offset = jnp.sum(jnp.where(ahead, mine.reshape(1, 1, -1), 0), axis=2)
    expert = (x * NZ + z) * NY + y
    limit = jnp.sum(jnp.where(jnp.arange(capacity.shape[0]) == expert, capacity, 0))
    kept = (offset[:, None, :] + ranks[None, :, None] < limit).reshape(rows, 1)

    def own_half(w, index, axis, size):
        return lax.dynamic_slice_in_dim(w, index * size, size, axis)

    gate_own, gate_sib = own_half(w_gate[0], hid, 0, width), own_half(w_gate[0], 1 - hid, 0, width)
    up_own, up_sib = own_half(w_up[0], hid, 0, width), own_half(w_up[0], 1 - hid, 0, width)
    down_own = own_half(w_down[0], hid, 1, width)
    down_sib = lax.ppermute(own_half(w_down[0], 1 - hid, 1, width), "hid", SWAP)

    stacked = jnp.concatenate(ring_gather(tokens), axis=0)
    outgoing = jnp.dot(pick, stacked, preferred_element_type=F32).astype(BF)
    received = lax.all_to_all(outgoing.reshape(planes, group, width), ("x", "y"), 0, 0, tiled=True)
    received = received.reshape(rows, width)
    other = lax.ppermute(received, "hid", SWAP)

    def dot(a, b):
        return jnp.dot(a, b, preferred_element_type=F32)

    gate_part = dot(received, gate_own) + dot(other, gate_sib)
    up_part = dot(received, up_own) + dot(other, up_sib)
    hidden = (jax.nn.silu(gate_part) * up_part).astype(BF)
    hidden_sib = lax.ppermute(hidden, "hid", SWAP)
    result = dot(hidden, down_own) + dot(hidden_sib, down_sib)
    result = jnp.where(kept, result, 0.0).astype(BF)

    returned = lax.all_to_all(result.reshape(planes, group, width), ("x", "y"), 0, 0, tiled=True)
    part = lax.dot_general(
        merge, returned.reshape(rows, width), (((0,), (0,)), ((), ())), preferred_element_type=F32
    ).reshape(NZ, tok, width)
    return ring_scatter(part).astype(BF)


def solution(mesh):
    wide = Mesh(mesh.devices.reshape(NX, NZ, NY, 2), ("x", "z", "y", "hid"))
    dp = ("x", "z", "y")
    in_specs = (
        P(dp, "hid"),
        P(dp, None),
        P(dp, None),
        P(),
        P(dp, None, "hid"),
        P(dp, None, "hid"),
        P(dp, "hid", None),
    )
    return jax.shard_map(
        on_device, mesh=wide, in_specs=in_specs, out_specs=P(dp, "hid"), check_vma=False
    )
```

```python
import jax
import jax.numpy as jnp
from jax import lax
from jax.sharding import Mesh, PartitionSpec as P

NX, NZ, NY = 4, 8, 4
SLOTS = 9
EMPTY = 64.0
BF = jnp.bfloat16
F32 = jnp.float32
SWAP = ((0, 1), (1, 0))
together = lax.optimization_barrier


def move(value, axis, size, by):
    return lax.ppermute(value, axis, [(i, (i + by) % size) for i in range(size)])


def hop(value, by):
    return move(value.astype(BF), "z", NZ, by).astype(F32)


def ring_scatter(part):
    half = part.shape[1] // 2
    far_down, far_up = hop(part[4, :half], -1), hop(part[4, half:], 1)
    down = jnp.concatenate([part[3, :half] + far_down, part[3, half:]], axis=0)
    up = jnp.concatenate([part[5, :half], part[5, half:] + far_up], axis=0)
    down = hop(down, -1) + part[2]
    up = hop(up, 1) + part[6]
    down = hop(down, -1) + part[1]
    up = hop(up, 1) + part[7]
    return (part[0] + hop(down, -1) + hop(up, 1)).astype(BF)


def dot(a, b):
    return jnp.dot(a, b, preferred_element_type=F32)


def on_device(tokens, routes, gates, capacity, w_gate, w_up, w_down):
    tok, width = tokens.shape
    planes = NX * NY
    group = SLOTS * NZ
    rows = planes * group
    units = w_gate.shape[2]
    x, z, y, hid = (lax.axis_index(a) for a in ("x", "z", "y", "hid"))
    experts = jnp.arange(planes, dtype=jnp.int32)
    back = jnp.arange(NZ, dtype=jnp.int32)
    ranks = jnp.arange(SLOTS, dtype=jnp.int32)
    row = jnp.arange(rows, dtype=jnp.int32)
    source_of = (z - back) % NZ

    def choose(first, second):
        return jnp.where(hid == 0, first, second)

    labels = jnp.concatenate([routes.astype(BF).T, gates.astype(BF).T], axis=0)
    labels = jnp.pad(labels, ((tok - 16, 0), (0, 0)))
    block = jnp.concatenate([tokens, labels], axis=1)
    up, down, half = [block], [block], tok // 2
    for step in range(3):
        up.append(move(up[-1], "z", NZ, 1))
        down.append(move(down[-1], "z", NZ, -1))
    far_up, far_down = move(up[3][half:], "z", NZ, 1), move(down[3][:half], "z", NZ, -1)
    metas = jnp.stack([b[-16:, width:] for b in [*up, far_up, *down[:0:-1]]])
    stacked = [b[:, :width] for b in [*up, far_down, far_up, *down[:0:-1]]]
    stacked = jnp.concatenate(stacked, axis=0)

    named_by = metas[:, :8].astype(jnp.int32)
    rounded = metas[:, 8:].astype(F32)
    expert_of = (experts // NY) * (NZ * NY) + z * NY + experts % NY
    named = named_by[None] == expert_of[:, None, None, None]
    mask = jnp.any(named, axis=2).astype(BF).reshape(planes * NZ, tok)
    factor = jnp.sum(jnp.where(named, rounded[None], 0.0), axis=2)
    before = (jnp.arange(tok)[:, None] < jnp.arange(tok)[None, :]).astype(BF)
    place = jnp.where(mask > 0, dot(mask, before), -1.0).reshape(planes, NZ, tok).astype(jnp.int32)
    same = back[:, None] == source_of[None, :]
    hit = (place[:, None, None] == ranks[None, :, None, None, None]) & same[None, None, :, :, None]
    pick = hit.astype(BF).reshape(rows, NZ * tok)
    pick, place, factor = together((pick, place, factor))
    filled = dot(pick, jnp.ones((NZ * tok, 128), BF))
    first_lane = jnp.arange(128)[None, :] == 0
    mark = jnp.where(first_lane & (filled == 0.0), EMPTY, 0.0)

    def exchange(value):
        value = value.reshape(planes, group, width)
        return lax.all_to_all(value, ("x", "y"), 0, 0, tiled=True).reshape(rows, width)

    picked = (dot(pick, stacked) + jnp.pad(mark, ((0, 0), (0, width - 128)))).astype(BF)
    picked, place, factor, w_gate, w_up, w_down = together(
        (picked, place, factor, w_gate, w_up, w_down)
    )
    received = exchange(picked)

    down_sib = lax.ppermute(choose(w_down[0][:, width:], w_down[0][:, :width]), "hid", SWAP)
    into_own = jnp.concatenate([choose(w[0][:width], w[0][width:]) for w in (w_gate, w_up)], axis=1)
    into_sib = jnp.concatenate([choose(w[0][width:], w[0][:width]) for w in (w_gate, w_up)], axis=1)
    out_of = choose(w_down[0][:, :width], w_down[0][:, width:])
    out_of = jnp.concatenate([out_of, down_sib], axis=0)
    order = (row // group // NY * NZ + row % NZ) * NY + row // group % NY
    ahead = (order[None, :] < order[:, None]).astype(BF)
    hit = (place[:, None, None] == ranks[None, :, None, None, None]) & same[None, None, :, :, None]
    merge = jnp.where(hit, factor[:, None, None], 0.0).astype(BF).reshape(rows, NZ * tok).T
    received, into_own, into_sib, out_of, ahead, merge = together(
        (received, into_own, into_sib, out_of, ahead, merge)
    )

    other = lax.ppermute(received, "hid", SWAP)
    both = dot(received, into_own)
    there = jnp.broadcast_to(received[:, :1] < EMPTY / 2, (rows, units))
    offset = dot(ahead, there.astype(BF))
    expert = (x * NZ + z) * NY + y
    limit = jnp.sum(jnp.where(jnp.arange(capacity.shape[0]) == expert, capacity, 0))
    rank = (row % group // NZ).astype(F32)[:, None]
    kept = (there & (offset + rank < limit.astype(F32))).astype(BF)
    other, both, kept = together((other, both, kept))
    both += dot(other, into_sib)
    gate_part, up_part = both[:, :units], both[:, units:]
    hidden = (jax.nn.silu(gate_part) * up_part * kept.astype(F32)).astype(BF)
    hidden = jnp.concatenate([hidden, lax.ppermute(hidden, "hid", SWAP)], axis=1)
    result = dot(hidden, out_of).astype(BF)

    returned = exchange(result)
    out, span = [], width // 2
    for h in range(2):
        part = dot(merge, returned[:, h * span : (h + 1) * span])
        out.append(ring_scatter(part.reshape(NZ, tok, span)))
    return jnp.concatenate(out, axis=1)


def solution(mesh):
    wide = Mesh(mesh.devices.reshape(NX, NZ, NY, 2), ("x", "z", "y", "hid"))
    dp = ("x", "z", "y")
    in_specs = (
        P(dp, "hid"),
        P(dp, None),
        P(dp, None),
        P(),
        P(dp, None, "hid"),
        P(dp, None, "hid"),
        P(dp, "hid", None),
    )
    return jax.shard_map(
        on_device, mesh=wide, in_specs=in_specs, out_specs=P(dp, "hid"), check_vma=False
    )
```

```python
import jax
import jax.numpy as jnp
from jax import lax
from jax.sharding import Mesh, PartitionSpec as P

NX, NZ, NY = 4, 8, 4
NEAR, FAR = (0, 1, 2, 6, 7), (3, 4, 5)
NEAR_ROWS, FAR_ROWS = 48, 32
EMPTY = 64.0
BF = jnp.bfloat16
F32 = jnp.float32
SWAP = ((0, 1), (1, 0))
together = lax.optimization_barrier


def move(value, axis, size, by):
    return lax.ppermute(value, axis, [(i, (i + by) % size) for i in range(size)])


def hop(value, by):
    return move(value.astype(BF), "z", NZ, by).astype(F32)


def dot(a, b):
    return jnp.dot(a, b, preferred_element_type=F32)


def on_device(tokens, routes, gates, capacity, w_gate, w_up, w_down):
    tok, width = tokens.shape
    planes = NX * NY
    units = w_gate.shape[2]
    half = tok // 2
    x, z, y, hid = (lax.axis_index(a) for a in ("x", "z", "y", "hid"))
    experts = jnp.arange(planes, dtype=jnp.int32)
    expert_of = (experts // NY) * (NZ * NY) + z * NY + experts % NY
    before = (jnp.arange(tok)[:, None] < jnp.arange(tok)[None, :]).astype(BF)

    def choose(first, second):
        return jnp.where(hid == 0, first, second)

    labels = jnp.concatenate([routes.astype(BF).T, gates.astype(BF).T], axis=0)
    labels = jnp.pad(labels, ((tok - 16, 0), (0, 0)))
    block = jnp.concatenate([tokens, labels], axis=1)
    up, down = [block], [block]
    for _ in range(3):
        up.append(move(up[-1], "z", NZ, 1))
        down.append(move(down[-1], "z", NZ, -1))
    far_up, far_down = move(up[3][half:], "z", NZ, 1), move(down[3][:half], "z", NZ, -1)

    def slots(blocks):
        metas = jnp.stack([b[-16:, width:] for b in blocks])
        named_by, rounded = metas[:, :8].astype(jnp.int32), metas[:, 8:].astype(F32)
        named = named_by[None] == expert_of[:, None, None, None]
        mask = jnp.any(named, axis=2).astype(BF)
        factor = jnp.sum(jnp.where(named, rounded[None], 0.0), axis=2)
        earlier = dot(mask.reshape(-1, tok), before).reshape(mask.shape)
        return jnp.where(mask > 0, earlier, -1.0).astype(jnp.int32), factor

    def hits(place, count):
        n = place.shape[1]
        row = jnp.arange(count, dtype=jnp.int32)
        ranked = place[:, None] == (row // n)[None, :, None, None]
        return ranked & (row[:, None] % n == jnp.arange(n)[None, :])[None, :, :, None]

    def select(place, count, blocks):
        pick = together(hits(place, count).astype(BF).reshape(planes * count, -1))
        filled = dot(pick, jnp.ones((pick.shape[1], 128), BF))
        mark = jnp.where((jnp.arange(128)[None, :] == 0) & (filled == 0.0), EMPTY, 0.0)
        picked = dot(pick, jnp.concatenate(blocks, axis=0))
        return (picked + jnp.pad(mark, ((0, 0), (0, width - 128)))).astype(BF)

    def weigh(place, factor, count):
        found = jnp.where(hits(place, count), factor[:, None], 0.0)
        return found.astype(BF).reshape(planes * count, -1).T

    def exchange(value):
        shape = value.shape
        value = value.reshape(planes, shape[0] // planes, shape[1])
        return lax.all_to_all(value, ("x", "y"), 0, 0, tiled=True).reshape(shape)

    def multiply(received, other):
        own, rest = dot(received, into_own), dot(other, into_sib)
        gate_part = own[:, :units] + rest[:, :units]
        return jax.nn.silu(gate_part) * (own[:, units:] + rest[:, units:])

    near = [up[0], up[1], up[2], down[2], down[1]]
    near_place, near_factor = slots(near)
    near_sent = select(near_place, NEAR_ROWS, [b[:, :width] for b in near])
    near_sent, w_gate, w_up, w_down = together((near_sent, w_gate, w_up, w_down))
    near_got = exchange(near_sent)

    far_place, far_factor = slots([up[3], far_up, down[3]])
    far_blocks = [b[:, :width] for b in (up[3], far_down, far_up, down[3])]
    far_sent = select(far_place, FAR_ROWS, far_blocks)
    into_own = jnp.concatenate([choose(w[0][:width], w[0][width:]) for w in (w_gate, w_up)], axis=1)
    into_sib = jnp.concatenate([choose(w[0][width:], w[0][:width]) for w in (w_gate, w_up)], axis=1)
    down_sib = lax.ppermute(choose(w_down[0][:, width:], w_down[0][:, :width]), "hid", SWAP)
    near_got, far_sent, into_own, into_sib, down_sib = together(
        (near_got, far_sent, into_own, into_sib, down_sib)
    )
    far_got = exchange(far_sent)

    near_hidden = multiply(near_got, lax.ppermute(near_got, "hid", SWAP)).astype(BF)
    near_hidden_other = lax.ppermute(near_hidden, "hid", SWAP)
    near_there = jnp.broadcast_to(near_got[:, :1] < EMPTY / 2, (near_got.shape[0], units)).astype(BF)
    near_merge = weigh(near_place, near_factor, NEAR_ROWS)
    far_merge = weigh(far_place, far_factor, FAR_ROWS)
    out_of = choose(w_down[0][:, :width], w_down[0][:, width:])
    out_of = jnp.concatenate([out_of, down_sib], axis=0)

    def order_of(backs, count):
        row = jnp.arange(planes * count, dtype=jnp.int32)
        q, r, i = row // count, row % count // len(backs), row % count % len(backs)
        back = sum(jnp.where(i == n, b, 0) for n, b in enumerate(backs))
        return (q // NY * NZ + (z - back) % NZ) * NY + q % NY, r

    near_order, near_rank = order_of(NEAR, NEAR_ROWS)
    far_order, far_rank = order_of(FAR, FAR_ROWS)
    order = jnp.concatenate([near_order, far_order])
    rank = jnp.concatenate([near_rank, far_rank]).astype(F32)[:, None]
    ahead = (order[None, :] < order[:, None]).astype(BF)
    far_got, near_hidden, near_hidden_other, near_there, near_merge, far_merge, out_of, ahead = together(
        (far_got, near_hidden, near_hidden_other, near_there, near_merge, far_merge, out_of, ahead)
    )

    far_other = lax.ppermute(far_got, "hid", SWAP)
    far_there = jnp.broadcast_to(far_got[:, :1] < EMPTY / 2, (far_got.shape[0], units)).astype(BF)
    there = jnp.concatenate([near_there, far_there], axis=0)
    expert = (x * NZ + z) * NY + y
    limit = jnp.sum(jnp.where(jnp.arange(capacity.shape[0]) == expert, capacity, 0))
    kept = ((there > 0) & (dot(ahead, there) + rank < limit.astype(F32))).astype(BF)
    split = near_got.shape[0]
    near_kept, far_kept = kept[:split], kept[split:]
    far_hidden = (multiply(far_got, far_other) * far_kept.astype(F32)).astype(BF)
    far_hidden = jnp.concatenate([far_hidden, lax.ppermute(far_hidden, "hid", SWAP)], axis=1)
    far_result = dot(far_hidden, out_of).astype(BF)

    far_result, near_kept = together((far_result, near_kept))
    far_back = exchange(far_result)
    near_hidden = jnp.concatenate([near_hidden * near_kept, near_hidden_other * near_kept], axis=1)
    near_result = dot(near_hidden, out_of).astype(BF)
    far_back, near_result = together((far_back, near_result))
    near_back = exchange(near_result)

    part3, part4, part5 = jnp.split(dot(far_merge, far_back), 3, axis=0)
    low, high = hop(part4[:half], -1), hop(part4[half:], 1)
    low = hop(jnp.concatenate([part3[:half] + low, part3[half:]], axis=0), -1)
    high = hop(jnp.concatenate([part5[:half], part5[half:] + high], axis=0), 1)
    near_back, low, high = together((near_back, low, high))
    part2, part6 = jnp.split(dot(near_merge[2 * tok : 4 * tok], near_back), 2, axis=0)
    low, high = hop(low + part2, -1), hop(high + part6, 1)
    part0, part1 = jnp.split(dot(near_merge[: 2 * tok], near_back), 2, axis=0)
    part7 = dot(near_merge[4 * tok :], near_back)
    return (part0 + hop(low + part1, -1) + hop(high + part7, 1)).astype(BF)


def solution(mesh):
    wide = Mesh(mesh.devices.reshape(NX, NZ, NY, 2), ("x", "z", "y", "hid"))
    dp = ("x", "z", "y")
    in_specs = (
        P(dp, "hid"),
        P(dp, None),
        P(dp, None),
        P(),
        P(dp, None, "hid"),
        P(dp, None, "hid"),
        P(dp, "hid", None),
    )
    return jax.shard_map(
        on_device, mesh=wide, in_specs=in_specs, out_specs=P(dp, "hid"), check_vma=False
    )
```

```python
import jax
import jax.numpy as jnp
import numpy as np
from jax import lax
from jax.sharding import Mesh, PartitionSpec as P

NX, NZ, NY = 4, 8, 4
BACKS = (0, 1, 2, 6, 7, 3, 4, 5)
NEAR_ROWS = np.array([(j % 5, j // 5) for j in range(40)])
FAR_ROWS = np.array([(5 + j % 3, j // 3) for j in range(27)] + [(j, 8) for j in range(5)])
EMPTY = 64.0
BF = jnp.bfloat16
F32 = jnp.float32
SWAP = ((0, 1), (1, 0))
together = lax.optimization_barrier


def move(value, axis, size, by):
    return lax.ppermute(value, axis, [(i, (i + by) % size) for i in range(size)])


def hop(value, by):
    return move(value.astype(BF), "z", NZ, by).astype(F32)


def dot(a, b):
    return jnp.dot(a, b, preferred_element_type=F32)


def on_device(tokens, routes, gates, capacity, w_gate, w_up, w_down):
    tok, width = tokens.shape
    planes = NX * NY
    units = w_gate.shape[2]
    half = tok // 2
    x, z, y, hid = (lax.axis_index(a) for a in ("x", "z", "y", "hid"))
    experts = jnp.arange(planes, dtype=jnp.int32)
    expert_of = (experts // NY) * (NZ * NY) + z * NY + experts % NY
    before = (jnp.arange(tok)[:, None] < jnp.arange(tok)[None, :]).astype(BF)

    def choose(first, second):
        return jnp.where(hid == 0, first, second)

    labels = jnp.concatenate([routes.astype(BF).T, gates.astype(BF).T], axis=0)
    labels = jnp.pad(labels, ((tok - 16, 0), (0, 0)))
    block = jnp.concatenate([tokens, labels], axis=1)
    up, down = [block], [block]
    for _ in range(3):
        up.append(move(up[-1], "z", NZ, 1))
        down.append(move(down[-1], "z", NZ, -1))
    far_up, far_down = move(up[3][half:], "z", NZ, 1), move(down[3][:half], "z", NZ, -1)

    def slots(blocks):
        metas = jnp.stack([b[-16:, width:] for b in blocks])
        named_by, rounded = metas[:, :8].astype(jnp.int32), metas[:, 8:].astype(F32)
        named = named_by[None] == expert_of[:, None, None, None]
        mask = jnp.any(named, axis=2).astype(BF)
        factor = jnp.sum(jnp.where(named, rounded[None], 0.0), axis=2)
        earlier = dot(mask.reshape(-1, tok), before).reshape(mask.shape)
        return jnp.where(mask > 0, earlier, -1.0).astype(jnp.int32), factor

    def hits(place, table):
        source, rank = jnp.asarray(table[:, 0], jnp.int32), jnp.asarray(table[:, 1], jnp.int32)
        ranked = place[:, None] == rank[None, :, None, None]
        return ranked & (source[:, None] == jnp.arange(place.shape[1])[None, :])[None, :, :, None]

    def select(place, table, blocks):
        pick = together(hits(place, table).astype(BF).reshape(planes * len(table), -1))
        filled = dot(pick, jnp.ones((pick.shape[1], 128), BF))
        mark = jnp.where((jnp.arange(128)[None, :] == 0) & (filled == 0.0), EMPTY, 0.0)
        picked, at = 0.0, 0
        for block in blocks:
            picked += dot(pick[:, at : at + block.shape[0]], block)
            at += block.shape[0]
        return (picked + jnp.pad(mark, ((0, 0), (0, width - 128)))).astype(BF)

    def weigh(place, factor, table):
        found = jnp.where(hits(place, table), factor[:, None], 0.0)
        return found.astype(BF).reshape(planes * len(table), -1).T

    def order_of(table):
        back = jnp.asarray(np.array(BACKS)[table[:, 0]], jnp.int32)[None, :]
        q = experts[:, None]
        rank = jnp.broadcast_to(jnp.asarray(table[:, 1], F32)[None, :], (planes, len(table)))
        order = (q // NY * NZ + (z - back) % NZ) * NY + q % NY
        return order.reshape(-1), rank.reshape(-1, 1)

    def there(got):
        return jnp.broadcast_to(got[:, :1] < EMPTY / 2, (got.shape[0], 128)).astype(BF)

    def ahead(first, second):
        return (second[None, :] < first[:, None]).astype(BF)

    def exchange(value):
        shape = value.shape
        value = value.reshape(planes, shape[0] // planes, shape[1])
        return lax.all_to_all(value, ("x", "y"), 0, 0, tiled=True).reshape(shape)

    def multiply(received, other):
        own, rest = dot(received, into_own), dot(other, into_sib)
        gate_part = own[:, :units] + rest[:, :units]
        return jax.nn.silu(gate_part) * (own[:, units:] + rest[:, units:])

    near = [up[0], up[1], up[2], down[2], down[1]]
    near_place, near_factor = slots(near)
    near_blocks = jnp.concatenate([b[:, :width] for b in near], axis=0)
    near_sent = select(near_place, NEAR_ROWS, [near_blocks])
    near_sent, near_blocks = together((near_sent, near_blocks))
    near_got = exchange(near_sent)

    far_up, far_down, w_gate, w_up, w_down = together((far_up, far_down, w_gate, w_up, w_down))
    place, factor = slots([up[3], far_up, down[3]])
    place = jnp.concatenate([near_place, place], axis=1)
    factor = jnp.concatenate([near_factor, factor], axis=1)
    far_blocks = jnp.concatenate([b[:, :width] for b in (up[3], far_down, far_up, down[3])], axis=0)
    far_sent = select(place, FAR_ROWS, [near_blocks, far_blocks])
    into_own = jnp.concatenate([choose(w[0][:width], w[0][width:]) for w in (w_gate, w_up)], axis=1)
    into_sib = jnp.concatenate([choose(w[0][width:], w[0][:width]) for w in (w_gate, w_up)], axis=1)
    down_sib = lax.ppermute(choose(w_down[0][:, width:], w_down[0][:, :width]), "hid", SWAP)
    near_got, far_sent, into_own, into_sib, down_sib = together(
        (near_got, far_sent, into_own, into_sib, down_sib)
    )
    far_got = exchange(far_sent)

    near_hidden = multiply(near_got, lax.ppermute(near_got, "hid", SWAP)).astype(BF)
    near_hidden_other = lax.ppermute(near_hidden, "hid", SWAP)
    near_merge = weigh(near_place, near_factor, NEAR_ROWS)
    far_merge = weigh(place, factor, FAR_ROWS)
    out_of = choose(w_down[0][:, :width], w_down[0][:, width:])
    out_of = jnp.concatenate([out_of, down_sib], axis=0)
    near_order, near_rank = order_of(NEAR_ROWS)
    far_order, far_rank = order_of(FAR_ROWS)
    near_there = there(near_got)
    near_rank += dot(ahead(near_order, near_order), near_there)
    far_rank += dot(ahead(far_order, near_order), near_there)
    near_ahead, far_ahead = ahead(near_order, far_order), ahead(far_order, far_order)
    expert = (x * NZ + z) * NY + y
    limit = jnp.sum(jnp.where(jnp.arange(capacity.shape[0]) == expert, capacity, 0)).astype(F32)
    beside = (into_own, into_sib, near_hidden, near_hidden_other, near_merge, far_merge, out_of)
    beside += (near_there, near_rank, far_rank, near_ahead, far_ahead, limit)
    far_got, beside = together((far_got, beside))
    into_own, into_sib, near_hidden, near_hidden_other, near_merge, far_merge, out_of = beside[:7]
    near_there, near_rank, far_rank, near_ahead, far_ahead, limit = beside[7:]

    far_other = lax.ppermute(far_got, "hid", SWAP)
    far_there = there(far_got)

    def keep(present, rank, order):
        kept = (present > 0) & (rank + dot(order, far_there) < limit)
        return jnp.concatenate([kept.astype(BF)] * (units // 128), axis=1)

    far_kept = keep(far_there, far_rank, far_ahead)
    near_kept = keep(near_there, near_rank, near_ahead)
    far_hidden = (multiply(far_got, far_other) * far_kept.astype(F32)).astype(BF)
    far_hidden = jnp.concatenate([far_hidden, lax.ppermute(far_hidden, "hid", SWAP)], axis=1)
    far_result = dot(far_hidden, out_of).astype(BF)

    far_result, near_kept = together((far_result, near_kept))
    far_back = exchange(far_result)
    near_hidden = jnp.concatenate([near_hidden * near_kept, near_hidden_other * near_kept], axis=1)
    near_result = dot(near_hidden, out_of).astype(BF)
    far_back, near_result = together((far_back, near_result))
    near_back = exchange(near_result)

    part3, part4, part5 = jnp.split(dot(far_merge[5 * tok :], far_back), 3, axis=0)
    low, high = hop(part4[:half], -1), hop(part4[half:], 1)
    low = hop(jnp.concatenate([part3[:half] + low, part3[half:]], axis=0), -1)
    high = hop(jnp.concatenate([part5[:half], part5[half:] + high], axis=0), 1)
    rest = dot(far_merge[: 5 * tok], far_back)
    near_back, low, high, rest = together((near_back, low, high, rest))

    def part(first, last):
        return dot(near_merge[first * tok : last * tok], near_back) + rest[first * tok : last * tok]

    part2, part6 = jnp.split(part(2, 4), 2, axis=0)
    low, high = hop(low + part2, -1), hop(high + part6, 1)
    part0, part1 = jnp.split(part(0, 2), 2, axis=0)
    return (part0 + hop(low + part1, -1) + hop(high + part(4, 5), 1)).astype(BF)


def solution(mesh):
    wide = Mesh(mesh.devices.reshape(NX, NZ, NY, 2), ("x", "z", "y", "hid"))
    dp = ("x", "z", "y")
    in_specs = (
        P(dp, "hid"),
        P(dp, None),
        P(dp, None),
        P(),
        P(dp, None, "hid"),
        P(dp, None, "hid"),
        P(dp, "hid", None),
    )
    return jax.shard_map(
        on_device, mesh=wide, in_specs=in_specs, out_specs=P(dp, "hid"), check_vma=False
    )
```

```python
import jax
import jax.numpy as jnp
import numpy as np
from jax import lax
from jax.sharding import Mesh, PartitionSpec as P

NX, NZ, NY = 4, 8, 4
BACKS = (0, 1, 2, 6, 7, 3, 4, 5)
NEAR_ROWS = np.array([(j % 5, j // 5) for j in range(40)])
FAR_ROWS = np.array([(5 + j % 3, j // 3) for j in range(27)] + [(j, 8) for j in range(5)])
EMPTY = 64.0
BF = jnp.bfloat16
F32 = jnp.float32
SWAP = ((0, 1), (1, 0))
together = lax.optimization_barrier


def move(value, axis, size, by):
    return lax.ppermute(value, axis, [(i, (i + by) % size) for i in range(size)])


def hop(value, by):
    return move(value.astype(BF), "z", NZ, by).astype(F32)


def dot(a, b):
    return jnp.dot(a, b, preferred_element_type=F32)


def on_device(tokens, routes, gates, capacity, w_gate, w_up, w_down):
    tok, width = tokens.shape
    planes = NX * NY
    units = w_gate.shape[2]
    half = tok // 2
    x, z, y, hid = (lax.axis_index(a) for a in ("x", "z", "y", "hid"))
    experts = jnp.arange(planes, dtype=jnp.int32)
    expert_of = (experts // NY) * (NZ * NY) + z * NY + experts % NY
    before = (jnp.arange(tok)[:, None] < jnp.arange(tok)[None, :]).astype(BF)

    def choose(first, second):
        return jnp.where(hid == 0, first, second)

    labels = jnp.concatenate([routes.astype(BF).T, gates.astype(BF).T], axis=0)
    labels = jnp.pad(labels, ((tok - 16, 0), (0, 0)))
    block = jnp.concatenate([tokens, labels], axis=1)
    up, down = [block], [block]
    for _ in range(3):
        up.append(move(up[-1], "z", NZ, 1))
        down.append(move(down[-1], "z", NZ, -1))
    far_up, far_down = move(up[3][half:], "z", NZ, 1), move(down[3][:half], "z", NZ, -1)

    def slots(blocks):
        metas = jnp.stack([b[-16:, width:] for b in blocks])
        named_by, rounded = metas[:, :8].astype(jnp.int32), metas[:, 8:].astype(F32)
        named = named_by[None] == expert_of[:, None, None, None]
        mask = jnp.any(named, axis=2).astype(BF)
        factor = jnp.sum(jnp.where(named, rounded[None], 0.0), axis=2)
        earlier = dot(mask.reshape(-1, tok), before).reshape(mask.shape)
        return jnp.where(mask > 0, earlier, -1.0).astype(jnp.int32), factor

    def hits(place, table):
        source, rank = jnp.asarray(table[:, 0], jnp.int32), jnp.asarray(table[:, 1], jnp.int32)
        ranked = place[:, None] == rank[None, :, None, None]
        return ranked & (source[:, None] == jnp.arange(place.shape[1])[None, :])[None, :, :, None]

    def select(place, table, blocks):
        pick = together(hits(place, table).astype(BF).reshape(planes * len(table), -1))
        filled = dot(pick, jnp.ones((pick.shape[1], 128), BF))
        mark = jnp.where((jnp.arange(128)[None, :] == 0) & (filled == 0.0), EMPTY, 0.0)
        picked, at = 0.0, 0
        for block in blocks:
            picked += dot(pick[:, at : at + block.shape[0]], block)
            at += block.shape[0]
        return (picked + jnp.pad(mark, ((0, 0), (0, width - 128)))).astype(BF)

    def weigh(place, factor, table):
        found = jnp.where(hits(place, table), factor[:, None], 0.0)
        return found.astype(BF).reshape(planes * len(table), -1).T

    def order_of(table):
        back = jnp.asarray(np.array(BACKS)[table[:, 0]], jnp.int32)[None, :]
        q = experts[:, None]
        rank = jnp.broadcast_to(jnp.asarray(table[:, 1], F32)[None, :], (planes, len(table)))
        order = (q // NY * NZ + (z - back) % NZ) * NY + q % NY
        return order.reshape(-1), rank.reshape(-1, 1)

    def there(got):
        return jnp.broadcast_to(got[:, :1] < EMPTY / 2, (got.shape[0], 128)).astype(BF)

    def ahead(first, second):
        return (second[None, :] < first[:, None]).astype(BF)

    def exchange(value):
        shape = value.shape
        value = value.reshape(planes, shape[0] // planes, shape[1])
        return lax.all_to_all(value, ("x", "y"), 0, 0, tiled=True).reshape(shape)

    def multiply(received, other):
        own, rest = dot(received, into_own), dot(other, into_sib)
        gate_part = own[:, :units] + rest[:, :units]
        return jax.nn.silu(gate_part) * (own[:, units:] + rest[:, units:])

    near = [up[0], up[1], up[2], down[2], down[1]]
    near_place, near_factor = slots(near)
    near_blocks = jnp.concatenate([b[:, :width] for b in near], axis=0)
    near_sent = select(near_place, NEAR_ROWS, [near_blocks])
    near_order, near_rank = order_of(NEAR_ROWS)
    far_order, far_rank = order_of(FAR_ROWS)
    maps = [ahead(f, n) for n in (near_order, far_order) for f in (near_order, far_order)]
    expert = (x * NZ + z) * NY + y
    limit = jnp.sum(jnp.where(jnp.arange(capacity.shape[0]) == expert, capacity, 0)).astype(F32)
    near_sent, near_blocks, maps, limit = together((near_sent, near_blocks, maps, limit))
    near_got = exchange(near_sent)

    far_up, far_down, w_gate, w_up, w_down = together((far_up, far_down, w_gate, w_up, w_down))
    place, factor = slots([up[3], far_up, down[3]])
    place = jnp.concatenate([near_place, place], axis=1)
    factor = jnp.concatenate([near_factor, factor], axis=1)
    far_blocks = jnp.concatenate([b[:, :width] for b in (up[3], far_down, far_up, down[3])], axis=0)
    far_sent = select(place, FAR_ROWS, [near_blocks, far_blocks])
    into_own = jnp.concatenate([choose(w[0][:width], w[0][width:]) for w in (w_gate, w_up)], axis=1)
    into_sib = jnp.concatenate([choose(w[0][width:], w[0][:width]) for w in (w_gate, w_up)], axis=1)
    down_sib = lax.ppermute(choose(w_down[0][:, width:], w_down[0][:, :width]), "hid", SWAP)
    near_got, far_sent, into_own, into_sib, down_sib = together(
        (near_got, far_sent, into_own, into_sib, down_sib)
    )
    far_got = exchange(far_sent)

    near_hidden = multiply(near_got, lax.ppermute(near_got, "hid", SWAP)).astype(BF)
    near_hidden_other = lax.ppermute(near_hidden, "hid", SWAP)
    near_merge = weigh(near_place, near_factor, NEAR_ROWS)
    far_merge = weigh(place, factor, FAR_ROWS)
    out_of = choose(w_down[0][:, :width], w_down[0][:, width:])
    out_of = jnp.concatenate([out_of, down_sib], axis=0)
    near_there = there(near_got)
    near_rank += dot(maps[0], near_there)
    far_rank += dot(maps[1], near_there)
    near_ahead, far_ahead = maps[2:]
    beside = (into_own, into_sib, near_hidden, near_hidden_other, near_merge, far_merge, out_of)
    beside += (near_there, near_rank, far_rank, near_ahead, far_ahead, limit)
    far_got, beside = together((far_got, beside))
    into_own, into_sib, near_hidden, near_hidden_other, near_merge, far_merge, out_of = beside[:7]
    near_there, near_rank, far_rank, near_ahead, far_ahead, limit = beside[7:]

    far_other = lax.ppermute(far_got, "hid", SWAP)
    far_there = there(far_got)

    def keep(present, rank, order):
        kept = (present > 0) & (rank + dot(order, far_there) < limit)
        return jnp.concatenate([kept.astype(BF)] * (units // 128), axis=1)

    far_kept = keep(far_there, far_rank, far_ahead)
    near_kept = keep(near_there, near_rank, near_ahead)
    far_hidden = (multiply(far_got, far_other) * far_kept.astype(F32)).astype(BF)
    far_hidden = jnp.concatenate([far_hidden, lax.ppermute(far_hidden, "hid", SWAP)], axis=1)
    far_result = dot(far_hidden, out_of).astype(BF)

    far_result, near_kept = together((far_result, near_kept))
    far_back = exchange(far_result)
    near_hidden = jnp.concatenate([near_hidden * near_kept, near_hidden_other * near_kept], axis=1)
    near_result = dot(near_hidden, out_of).astype(BF)
    far_back, near_result = together((far_back, near_result))
    near_back = exchange(near_result)

    part3, part4, part5 = jnp.split(dot(far_merge[5 * tok :], far_back), 3, axis=0)
    low, high = hop(part4[:half], -1), hop(part4[half:], 1)
    low = hop(jnp.concatenate([part3[:half] + low, part3[half:]], axis=0), -1)
    high = hop(jnp.concatenate([part5[:half], part5[half:] + high], axis=0), 1)
    rest = dot(far_merge[: 5 * tok], far_back)
    near_back, low, high, rest = together((near_back, low, high, rest))

    def part(first, last):
        return dot(near_merge[first * tok : last * tok], near_back) + rest[first * tok : last * tok]

    part2, part6 = jnp.split(part(2, 4), 2, axis=0)
    low, high = hop(low + part2, -1), hop(high + part6, 1)
    part0, part1 = jnp.split(part(0, 2), 2, axis=0)
    return (part0 + hop(low + part1, -1) + hop(high + part(4, 5), 1)).astype(BF)


def solution(mesh):
    wide = Mesh(mesh.devices.reshape(NX, NZ, NY, 2), ("x", "z", "y", "hid"))
    dp = ("x", "z", "y")
    in_specs = (
        P(dp, "hid"),
        P(dp, None),
        P(dp, None),
        P(),
        P(dp, None, "hid"),
        P(dp, None, "hid"),
        P(dp, "hid", None),
    )
    return jax.shard_map(
        on_device, mesh=wide, in_specs=in_specs, out_specs=P(dp, "hid"), check_vma=False
    )
```
